256 devices in a mesh: role: 4 (over x_lo, core), seq: 16 (over x_hi, z), tp: 4 (over y).
Axes of the slice: x: 4 (x_hi: 2, x_lo: 2; x = x_hi * 2 + x_lo), y: 4, z: 8, core: 2. Of those that a mesh axis runs over, the one named last changes fastest.
Arguments:
- gen_input: bfloat16 [2048, 64], P('seq'), may hold values from -6 to 6
- generated: bfloat16 [2048, 64], P('seq'), may hold values from -6 to 6
- noise: bfloat16 [2048, 64], P('seq'), may hold values from -6 to 6
- timesteps: int32 [7], replicated, may hold values from 20 to 979
- block_lengths: int32 [7], replicated, may hold values from 1 to 512, 2048 in all
- w_embed: bfloat16 [3, 5120, 64], P(None, 'seq'), may hold values from -0.75 to 0.75
- w_qkv: bfloat16 [3, 5120, 20, 3, 128], P(None, 'seq', 'tp')
- w_out: bfloat16 [3, 20, 128, 64], P(None, 'tp'), may hold values from -0.125 to 0.125
- modulation: float32 [4, 2, 5120], P('role'), may hold values from -3 to 3
Outputs:
- velocities: bfloat16 [4, 2048, 64], P('role', 'seq')
- qkv_grads: bfloat16 [4, 2048, 20, 3, 128], P('role', 'seq', 'tp')
The draws below stay inside these ranges and needn't reach their ends.
Inputs may be any that keep to these rules, and one draw needn't show every extreme that they name: `block_lengths`: the block lengths sum to 2048; the longest is exactly 512.
All inputs are finite; a program needn't handle non-finite values. Where the reference program divides by a largest or mean magnitude, that divisor is 1e-20 or more.
Results may differ from the reference program's by a relative error of at most 0.02.
Values may be sent and summed in bfloat16 or wider, within the bound.
A program may use at most 128 MiB of HBM per device.

```python
import math
import jax
import jax.numpy as jnp
import numpy as np
from jax import lax

D = 5120
HEADS = 20
HEAD = 128
C = 64
NETS = 3
BLOCKS = 7
TOKENS = 2048
N_ROLE = 4


def draw_w_qkv(key, part):
    key = jax.random.fold_in(key, 11)
    shape = (NETS, D, HEADS, 3, HEAD)
    spread = 1.5 / math.sqrt(D)
    base = jax.random.normal(key, shape, jnp.float32) * spread
    return base.astype(jnp.bfloat16)


def plant(values, rng, low, largest):
    index_at = [jax.random.randint(jax.random.fold_in(rng, axis), (), 0, length) for axis, length in enumerate(values.shape)]
    longest = values.shape.index(max(values.shape))
    neighbour = index_at[:longest] + [(index_at[longest] + 1) % values.shape[longest]] + index_at[longest + 1:]
    return values.at[tuple(index_at)].set(low).at[tuple(neighbour)].set(largest)


def shard_levels(key, extent, cuts, low, largest):
    def one(dim, blocks):
        draws = jax.random.uniform(jax.random.fold_in(jax.random.fold_in(key, 6), dim), (blocks,), jnp.float32, low / len(cuts), largest / len(cuts))
        return jnp.repeat(jnp.exp(draws), extent[dim] // blocks).reshape((-1,) + (1,) * (len(extent) - dim - 1))

    factor_of = one(*cuts[0])
    for cut in cuts[1:]:
        factor_of = factor_of * one(*cut)
    return factor_of


def length_profile(count, total, reach, lean):
    weights = [(1 << 20) // math.isqrt(grade ** lean) + 1 for grade in range(2, count + 1)]
    spare, counts = total - reach - (count - 1), [1] * (count - 1)
    while spare > 0:
        movable = [i for i in range(count - 1) if counts[i] < reach]
        mass, budget = sum([weights[i] for i in movable]), spare
        for i in movable:
            extra = min(reach - counts[i], max(1, budget * weights[i] // mass), spare)
            counts[i] = counts[i] + extra
            spare = spare - extra
    return np.array([reach] + counts)


def ragged(rng, number_of, total, most, lean):
    if number_of == 2:
        one = jax.random.randint(rng, (), max(1, total - most), min(most, total - 1) + 1)
        return jnp.stack([one, total - one])
    tallies = jnp.asarray(length_profile(number_of, total, most, lean), jnp.int32)
    couples = (number_of - 1) // 2
    donor, receiver = tallies[1:1 + 2 * couples:2], tallies[2:2 + 2 * couples:2]
    slack = jnp.minimum(donor - 1, most - receiver)
    moved = jax.random.randint(jax.random.fold_in(rng, 1), (couples,), 0, 1 << 20) % (slack + 1)
    tallies = tallies.at[1:1 + 2 * couples:2].set(donor - moved).at[2:2 + 2 * couples:2].set(receiver + moved)
    return tallies[jax.random.permutation(jax.random.fold_in(rng, 2), number_of)]


def normal_values(own_key, dims, scale, most, cuts=(), held_as=jnp.bfloat16):
    result = scale * jax.random.normal(own_key, dims, jnp.float32)
    if cuts:
        result = result * shard_levels(own_key, dims, cuts, -0.22, 0.18)
    return jnp.clip(result, -most, most).astype(held_as)


def setup_inputs(seed: int = 0) -> dict:
    streams_of = jax.random.split(jax.random.key(seed), 10)
    return {
        "gen_input": normal_values(streams_of[0], (TOKENS, C), 1.0, 6.0, ((0, 16),)),
        "generated": normal_values(streams_of[1], (TOKENS, C), 1.0, 6.0, ((0, 16),)),
        "noise": normal_values(streams_of[2], (TOKENS, C), 1.0, 6.0, ((0, 16),)),
        "timesteps": plant(jax.random.randint(streams_of[3], (BLOCKS,), 20, 980), jax.random.fold_in(streams_of[3], 1), 20, 979).astype(jnp.int32),
        "block_lengths": ragged(streams_of[4], BLOCKS, TOKENS, TOKENS // 4, 1).astype(jnp.int32),
        "w_embed": normal_values(streams_of[5], (NETS, D, C), C ** -0.5, 0.75, ((1, 16),)),
        "w_qkv": draw_w_qkv(jax.random.fold_in(streams_of[9], 71), 0),
        "w_out": normal_values(streams_of[7], (NETS, HEADS, HEAD, C), (HEADS * HEAD) ** -0.5, 0.125, ((1, 4),)),
        "modulation": normal_values(streams_of[8], (N_ROLE, 2, D), 0.5, 3.0, ((0, 4),), jnp.float32),
    }


eps_norm = 1e-06
masked_value = -1e+30
guide_scale = 5.0

def block_index(positions, block_ends):
    return lax.optimization_barrier(jnp.sum((positions[:, None] >= block_ends[None, :]).astype(jnp.int32), axis=1))

def noise_level(block_ids, timesteps):
    picks = (block_ids[:, None] == jnp.arange(BLOCKS, dtype=jnp.int32)[None, :]).astype(jnp.float32)
    return lax.optimization_barrier(jnp.sum(picks * timesteps.astype(jnp.float32)[None, :], axis=1)) / 1000.0

def head_probs(queries, keys_head, allowed):
    scores = jnp.dot(queries, keys_head.T, preferred_element_type=jnp.float32) * HEAD ** (-0.5)
    scores = jnp.where(allowed, scores, masked_value)
    top_score = lax.optimization_barrier(jnp.max(scores, axis=1, keepdims=True))
    weights = jnp.exp(scores - top_score)
    return weights / lax.optimization_barrier(jnp.sum(weights, axis=1, keepdims=True))

def head_forward(pieces, allowed):
    queries, keys_head, values_head = pieces
    probs = head_probs(queries, keys_head, allowed)
    return jnp.dot(probs.astype(jnp.bfloat16), values_head, preferred_element_type=jnp.float32).astype(jnp.bfloat16)

def head_backward(pieces, allowed):
    queries, keys_head, values_head, attended, grad_attended = pieces
    probs = head_probs(queries, keys_head, allowed)
    row_delta = lax.optimization_barrier(jnp.sum(grad_attended.astype(jnp.float32) * attended.astype(jnp.float32), axis=1, keepdims=True))
    grad_probs = jnp.dot(grad_attended, values_head.T, preferred_element_type=jnp.float32)
    grad_scores = (probs * (grad_probs - row_delta) * HEAD ** (-0.5)).astype(jnp.bfloat16)
    grad_query = jnp.dot(grad_scores, keys_head, preferred_element_type=jnp.float32).astype(jnp.bfloat16)
    grad_key = jnp.dot(grad_scores.T, queries, preferred_element_type=jnp.float32).astype(jnp.bfloat16)
    grad_value = jnp.dot(probs.astype(jnp.bfloat16).T, grad_attended, preferred_element_type=jnp.float32).astype(jnp.bfloat16)
    return jnp.stack([grad_query, grad_key, grad_value], axis=1)

def network(latents, embed_rows, qkv_weight, out_weight, modulate, allowed):
    embedded = jnp.dot(latents, embed_rows.T, preferred_element_type=jnp.float32)
    mean_square = lax.optimization_barrier(jnp.mean(embedded * embedded, axis=1, keepdims=True))
    normed = (embedded * lax.rsqrt(mean_square + eps_norm) * (1.0 + modulate[0]) + modulate[1]).astype(jnp.bfloat16)
    projected = jnp.dot(normed, qkv_weight.reshape(D, HEADS * 3 * HEAD), preferred_element_type=jnp.float32).astype(jnp.bfloat16)
    projected = projected.reshape(TOKENS, HEADS, 3, HEAD).transpose(1, 2, 0, 3)
    attended = lax.map(lambda piece: head_forward(piece, allowed), (projected[:, 0], projected[:, 1], projected[:, 2]))
    flat = attended.transpose(1, 0, 2).reshape(TOKENS, HEADS * HEAD)
    velocity = jnp.dot(flat, out_weight.reshape(HEADS * HEAD, C), preferred_element_type=jnp.float32).astype(jnp.bfloat16)
    return (velocity, projected, attended)

def backward(projected, attended, cotangent, out_weight, allowed):
    grad_flat = jnp.dot(cotangent, out_weight.reshape(HEADS * HEAD, C).T, preferred_element_type=jnp.float32).astype(jnp.bfloat16)
    grad_heads = grad_flat.reshape(TOKENS, HEADS, HEAD).transpose(1, 0, 2)
    grads = lax.map(lambda piece: head_backward(piece, allowed), (projected[:, 0], projected[:, 1], projected[:, 2], attended, grad_heads))
    return grads.transpose(1, 0, 2, 3)

def reference(gen_input, generated, noise, timesteps, block_lengths, w_embed, w_qkv, w_out, modulation):
    positions = jnp.arange(TOKENS, dtype=jnp.int32)
    block_ends = jnp.cumsum(block_lengths).astype(jnp.int32)
    block_ids = block_index(positions, block_ends)
    allowed = block_ids[None, :] <= block_ids[:, None]
    sigma = noise_level(block_ids, timesteps)[:, None]
    clean = generated.astype(jnp.float32)
    fresh = noise.astype(jnp.float32)
    noised = ((1.0 - sigma) * clean + sigma * fresh).astype(jnp.bfloat16)
    net_of_role = (0, 1, 1, 2)
    velocities = []
    saved = []
    for role_index in range(4):
        latents = gen_input if role_index == 0 else noised
        net_index = net_of_role[role_index]
        velocity, projected, attended = network(latents, w_embed[net_index], w_qkv[net_index], w_out[net_index], modulation[role_index], allowed)
        velocities.append(velocity)
        saved.append((projected, attended))
    with_prompt = velocities[1].astype(jnp.float32)
    without_prompt = velocities[2].astype(jnp.float32)
    fake_velocity = velocities[3].astype(jnp.float32)
    real_velocity = without_prompt + guide_scale * (with_prompt - without_prompt)
    noised_wide = noised.astype(jnp.float32)
    real_clean = noised_wide - sigma * real_velocity
    fake_clean = noised_wide - sigma * fake_velocity
    spread = jnp.mean(jnp.abs(clean - real_clean)) + eps_norm
    dmd_cotangent = ((fake_clean - real_clean) / spread).astype(jnp.bfloat16)
    critic_cotangent = (fake_velocity - (fresh - clean)).astype(jnp.bfloat16)
    grad_first = backward(saved[0][0], saved[0][1], dmd_cotangent, w_out[0], allowed)
    grad_last = backward(saved[3][0], saved[3][1], critic_cotangent, w_out[2], allowed)
    nothing = jnp.zeros_like(grad_first)
    return (jnp.stack(velocities), jnp.stack([grad_first, nothing, nothing, grad_last]))
```

```python
import functools
import math

import jax
import jax.numpy as jnp
from jax import lax
from jax.experimental import pallas as pl
from jax.experimental.pallas import tpu as pltpu
from jax.sharding import PartitionSpec as P

MESH = pl.DeviceIdType.MESH
F32 = jnp.float32
BF16 = jnp.bfloat16

eps_norm = 1e-06
masked_value = -1e30
guide_scale = 5.0

ROWS = 160
ONE_A = 128
MARK = 129
ONE_B = 136
SIDE = 16


def nn(a, b):
    return lax.dot_general(a, b, (((1,), (0,)), ((), ())), preferred_element_type=F32)


def nt(a, b):
    return lax.dot_general(a, b, (((1,), (1,)), ((), ())), preferred_element_type=F32)


def iota(shape, dim):
    return lax.broadcasted_iota(jnp.int32, shape, dim)


def kernel(
    seq_count, tp_count, x_hi,
    gen_hbm, clean_hbm, fresh_hbm, steps_hbm, lens_hbm, emb_hbm, qkv_hbm, out_hbm, mod_hbm,
    vel, grads,
    gen, clean, fresh, steps, lens, mod, emb, wq, wo, lhs, part, rs, mall, ylocal, ybuf, slabs, mext,
    lq, lk, lv, lg, s_ref, p_ref, t1, u1, uk, uv, mx, vb, xb, zc, zl, cot_ref,
    load_sem, y_send, y_recv, w_send, w_recv, rs_send, rs_recv, ag_send, ag_recv,
    zc_send, zc_recv, zl_send, zl_recv, v_send, v_recv, x_send, x_recv,
):
    role = lax.axis_index("role")
    me = lax.axis_index("seq")
    tp = lax.axis_index("tp")
    channels, tok = gen.shape
    feats = emb.shape[1]
    heads, _, head = wo.shape
    blocks = lens.shape[0]
    every = seq_count * tok
    net = lax.div(role + 1, 2)
    per_chunk = s_ref.shape[2] // tok
    chunks = seq_count // per_chunk
    z_len = seq_count // x_hi
    my_x, my_z = lax.div(me, z_len), lax.rem(me, z_len)
    last = 3 * heads

    def at_offset(dx, dz):
        return lax.rem(my_x + dx, x_hi) * z_len + lax.rem(my_z + dz, z_len)

    def far_first(k):
        dx = 1 - lax.rem(k, 2)
        half = lax.div(k, 2)
        dz = z_len // 2 + (1 - 2 * lax.rem(half, 2)) * lax.div(half + 1, 2)
        return at_offset(dx, dz)

    def early_first(k):
        kind = lax.rem(my_z + lax.div(k, seq_count // 2), 2)
        j = lax.rem(k, seq_count // 2)
        dx = 1 - lax.rem(j, 2)
        half = lax.div(j, 2)
        even = z_len // 2 + 2 * (1 - 2 * lax.rem(half, 2)) * lax.div(half + 1, 2)
        odd = z_len // 2 - (1 - 2 * lax.rem(half, 2)) * (2 * lax.div(half, 2) + 1)
        return at_offset(dx, (1 - kind) * even + kind * odd)

    def block_at(who):
        x, z = lax.div(who, z_len), lax.rem(who, z_len)
        place = x * (z_len // 2) + lax.div(z, 2)
        first = place + lax.div(place, seq_count // 2 - 1) * (last - (seq_count // 2 - 1))
        late = lax.rem(z, 2)
        return (1 - late) * first + late * (place + seq_count // 2 - 1)

    def owner_of(b):
        half = seq_count // 2
        place, late = (half - 1, 0) if b == last else ((b, 0) if b < half - 1 else (b - half + 1, 1))
        return place // (z_len // 2) * z_len + 2 * (place % (z_len // 2)) + late

    my_block = block_at(me)

    barrier = pltpu.get_barrier_semaphore()

    def greet_seq(k, carry):
        pl.semaphore_signal(barrier, inc=1, device_id={"seq": far_first(k)}, device_id_type=MESH)
        return carry

    lax.fori_loop(0, seq_count - 1, greet_seq, 0)
    for d in range(1, tp_count):
        pl.semaphore_signal(barrier, inc=1, device_id={"tp": lax.rem(tp + d, tp_count)}, device_id_type=MESH)

    @pl.when(role == 0)
    def _():
        for other in range(1, 4):
            for t in range(tp_count):
                pl.semaphore_signal(barrier, inc=1, device_id={"role": other, "tp": t}, device_id_type=MESH)

    feat_start = pl.multiple_of(lax.div(me * feats, 128) * 128, 128)
    sources = (
        (emb_hbm.at[net], emb), (mod_hbm.at[:, pl.ds(feat_start, mod.shape[1])], mod), (steps_hbm, steps), (lens_hbm, lens),
        (gen_hbm, gen), (clean_hbm, clean), (fresh_hbm, fresh), (qkv_hbm.at[net], wq), (out_hbm.at[net], wo),
    )
    loads = [pltpu.make_async_copy(src, dst, load_sem.at[i]) for i, (src, dst) in enumerate(sources)]
    for load in loads:
        load.start()
    for load in loads[2:7]:
        load.wait()

    ends = []
    total = jnp.int32(0)
    for j in range(blocks):
        total = total + lens[j]
        ends.append(total)

    def block_of(positions):
        ids = jnp.zeros_like(positions)
        for j in range(blocks):
            ids = ids + (positions >= ends[j]).astype(jnp.int32)
        return ids

    lane_block = block_of(me * tok + iota((1, tok), 1))
    sigma = jnp.zeros((1, tok), F32)
    for j in range(blocks):
        sigma = sigma + jnp.where(lane_block == j, steps[j].astype(F32), 0.0)
    sigma = sigma / 1000.0
    clean32 = clean[...].astype(F32)
    fresh32 = fresh[...].astype(F32)
    noised = ((1.0 - sigma) * clean32 + sigma * fresh32).astype(BF16)
    latents = jnp.where(role == 0, gen[...].astype(F32), noised.astype(F32)).astype(BF16)
    quarter = channels // tp_count
    for t in range(tp_count):
        ylocal[t] = latents[t * quarter : (t + 1) * quarter]
    ybuf[tp, me] = ylocal[tp]

    @pl.when(role == 0)
    def _():
        pl.semaphore_wait(barrier, seq_count - 1 + tp_count - 1)

    @pl.when(role != 0)
    def _():
        pl.semaphore_wait(barrier, seq_count - 1 + tp_count - 1 + tp_count)

    def over_seq(src, dst, send, recv, order=far_first):
        def copy(who):
            return pltpu.make_async_remote_copy(
                src_ref=src(who), dst_ref=dst(me, who), send_sem=send.at[who], recv_sem=recv.at[me],
                device_id={"seq": who}, device_id_type=MESH,
            )

        def start():
            def body(k, carry):
                who = order(k)

                @pl.when(who != me)
                def _():
                    copy(who).start()

                return carry

            lax.fori_loop(0, seq_count, body, 0)

        def wait_sent():
            def body(k, carry):
                copy(far_first(k)).wait_send()
                return carry

            lax.fori_loop(0, seq_count - 1, body, 0)

        def wait_from(who):
            pltpu.make_async_remote_copy(
                src_ref=dst(who, me), dst_ref=dst(who, me), send_sem=send.at[who], recv_sem=recv.at[who],
                device_id={"seq": who}, device_id_type=MESH,
            ).wait_recv()

        def wait_all():
            def body(k, carry):
                wait_from(far_first(k))
                return carry

            lax.fori_loop(0, seq_count - 1, body, 0)

        return start, wait_sent, wait_from, wait_all

    y_start, y_wait_sent, _, y_wait_all = over_seq(
        lambda who: ybuf.at[tp, me], lambda who, at: ybuf.at[tp, who], y_send, y_recv
    )
    zc_start, zc_wait_sent, zc_wait_from, _ = over_seq(lambda who: zc.at[me], lambda who, at: zc.at[who], zc_send, zc_recv)
    zl_start, zl_wait_sent, zl_wait_from, _ = over_seq(lambda who: zl.at[me], lambda who, at: zl.at[who], zl_send, zl_recv)
    y_start()

    def rs_copy(who, rows):
        return pltpu.make_async_remote_copy(
            src_ref=part.at[block_at(who), 0:rows], dst_ref=rs.at[me, 0:rows], send_sem=rs_send.at[who],
            recv_sem=rs_recv.at[me], device_id={"seq": who}, device_id_type=MESH,
        )

    def rs_arrival(who, rows):
        return pltpu.make_async_remote_copy(
            src_ref=rs.at[who, 0:rows], dst_ref=rs.at[who, 0:rows], send_sem=rs_send.at[who],
            recv_sem=rs_recv.at[who], device_id={"seq": who}, device_id_type=MESH,
        )

    def ag_copy(who, rows):
        mine = mall.at[my_block, 0:rows]
        return pltpu.make_async_remote_copy(
            src_ref=mine, dst_ref=mine, send_sem=ag_send.at[who], recv_sem=ag_recv.at[me],
            device_id={"seq": who}, device_id_type=MESH,
        )

    long_rows, short_rows = channels + 16, channels

    def by_length(is_long, action):
        @pl.when(is_long)
        def _():
            action(long_rows)

        @pl.when(jnp.logical_not(is_long))
        def _():
            action(short_rows)

    def ag_wait(b):
        owner = owner_of(b)
        there = mall.at[b, 0 : long_rows if b == last else short_rows]

        @pl.when(me != owner)
        def _():
            pltpu.make_async_remote_copy(
                src_ref=there, dst_ref=there, send_sem=ag_send.at[owner], recv_sem=ag_recv.at[owner],
                device_id={"seq": owner}, device_id_type=MESH,
            ).wait_recv()

    loads[0].wait()
    loads[1].wait()
    odd = lax.rem(me, 2) == 1
    window = mod[...]
    mine = jnp.where(odd, window[:, 64 : 64 + feats], window[:, :feats])
    scale, shift = 1.0 + mine[0:1], mine[1:2]
    emb_now = emb[...]
    scaled = emb_now.astype(F32) * scale
    scaled_hi = scaled.astype(BF16)
    shift_rows = jnp.where(iota((16, feats), 0) == 0, shift, 0.0)
    shift_hi = shift_rows.astype(BF16)
    lhs[0:64, :] = scaled_hi
    lhs[64:80, :] = shift_hi
    lhs[80:144, :] = (scaled - scaled_hi.astype(F32)).astype(BF16)
    lhs[144:160, :] = (shift_rows - shift_hi.astype(F32)).astype(BF16)
    gram = nt(emb_now, jnp.concatenate([emb_now, emb_now], axis=0))
    gram_hi = gram.astype(BF16).astype(F32)
    left_half = iota((channels, 2 * channels), 1) < channels
    part[last, 0:64, :] = jnp.where(left_half, gram_hi, gram - gram_hi).astype(BF16)
    loads[7].wait()
    lhs_now = lhs[...]
    bias = jnp.zeros((16, head), F32)
    bias_row = iota((16, head), 0)
    for b in range(last):
        both = nn(lhs_now, wq[b // 3, b % 3])
        both = both[0:80] + both[80:160]
        part[b, 0:64, :] = both[0:64].astype(BF16)
        bias = jnp.where(bias_row == b, both[64:65], bias)
    part[last, 64:80, :] = bias.astype(BF16)
    rs[me] = part[my_block]

    def rs_step(k, carry):
        who = early_first(k)

        @pl.when(who != me)
        def _():
            by_length(block_at(who) == last, lambda rows: rs_copy(who, rows).start())

        return carry

    lax.fori_loop(0, seq_count, rs_step, 0)

    row_id = iota((16, every), 0)
    wide_block = block_of(iota((1, every), 1))
    extras = jnp.where(
        (row_id == 0) | (row_id == ONE_B - ONE_A) | ((row_id < ONE_B - ONE_A) & (wide_block == row_id - 1)), 1.0, 0.0
    ).astype(BF16)
    for s in range(seq_count):
        slabs[s, 128:144, :] = extras[:, s * tok : (s + 1) * tok]
        slabs[s, 144:160, :] = jnp.zeros((16, tok), BF16)

    y_wait_all()

    def quarter_copy(d):
        other = lax.rem(tp + d, tp_count)
        return pltpu.make_async_remote_copy(
            src_ref=ybuf.at[tp], dst_ref=ybuf.at[tp], send_sem=w_send.at[other], recv_sem=w_recv.at[tp],
            device_id={"tp": other}, device_id_type=MESH,
        )

    def quarter_arrival(d):
        other = lax.rem(tp + d, tp_count)
        return pltpu.make_async_remote_copy(
            src_ref=ybuf.at[other], dst_ref=ybuf.at[other], send_sem=w_send.at[other], recv_sem=w_recv.at[other],
            device_id={"tp": other}, device_id_type=MESH,
        )

    for d in (2, 1, 3):
        quarter_copy(d).start()

    def rs_wait(k, carry):
        who = far_first(k)
        by_length(my_block == last, lambda rows: rs_arrival(who, rows).wait_recv())
        return carry

    lax.fori_loop(0, seq_count - 1, rs_wait, 0)
    owned = jnp.zeros((64, 128), F32)
    for s in range(seq_count):
        owned = owned + rs[s, 0:64, :].astype(F32)
    folded = owned + pltpu.roll(owned, 64, 1)
    folded_hi = folded.astype(BF16).astype(F32)
    half = jnp.where(left_half, folded_hi, folded - folded_hi)
    mall[my_block, 0:64, :] = jnp.where(my_block == last, half, owned).astype(BF16)

    @pl.when(my_block == last)
    def _():
        owned_bias = jnp.zeros((16, 128), F32)
        for s in range(seq_count):
            owned_bias = owned_bias + rs[s, 64:80, :].astype(F32)
        mall[last, 64:80, :] = owned_bias.astype(BF16)

    def ag_step(k, carry):
        who = far_first(k)
        by_length(my_block == last, lambda rows: ag_copy(who, rows).start())
        return carry

    lax.fori_loop(0, seq_count - 1, ag_step, 0)

    for d in (2, 1, 3):
        quarter_arrival(d).wait_recv()
    ag_wait(last)
    y_all = jnp.concatenate(
        [jnp.concatenate([ybuf[t, s] for t in range(tp_count)], axis=0) for s in range(seq_count)], axis=1
    )
    y_wide = y_all.astype(F32)
    gram_y = nn(mall[last, 0:64, :], jnp.concatenate([y_all, y_all], axis=0))
    mean_square = jnp.sum(gram_y * y_wide, axis=0, keepdims=True) / (feats * seq_count)
    ry = y_wide * lax.rsqrt(jnp.maximum(mean_square, 0.0) + eps_norm)
    ry_hi = ry.astype(BF16)
    ry_lo = (ry - ry_hi.astype(F32)).astype(BF16)
    for s in range(seq_count):
        slabs[s, 0:64, :] = ry_hi[:, s * tok : (s + 1) * tok]
        slabs[s, 64:128, :] = ry_lo[:, s * tok : (s + 1) * tok]

    loads[8].wait()
    y_tok = jnp.transpose(slabs[me].astype(F32)).astype(BF16)
    tok_block = block_of(me * tok + iota((tok, ROWS), 0))
    lane = iota((tok, ROWS), 1)
    in_marks = (lane >= MARK) & (lane < MARK + blocks)
    later_keys = jnp.where(in_marks & (lane - MARK > tok_block), masked_value, 0.0)
    earlier_queries = jnp.where(in_marks & (lane - MARK < tok_block), masked_value, 0.0)
    root_scale = math.log2(math.e) / math.sqrt(head)
    inv_root = 1.0 / math.sqrt(head)
    first_row = iota((16, head), 0) == 0
    zlane = iota((tok, channels + SIDE), 1)
    side_lane = iota((tok, SIDE), 1)

    def split_const(rows, extra, const):
        low = const - const.astype(BF16).astype(F32)
        return jnp.where(lane == ONE_B, low, jnp.where(lane == ONE_A, const, rows + extra)).astype(BF16)

    def extend(b):
        mext[b, 0:64, :] = mall[b, 0:64, :]
        mext[b, 64:128, :] = mall[b, 0:64, :]
        mext[b, 128:144, :] = jnp.where(first_row, mall[last, 64:80, :].astype(F32)[b : b + 1], 0.0).astype(BF16)
        mext[b, 144:160, :] = jnp.zeros((16, head), BF16)

    def project(h):
        here = slice(h * tok, (h + 1) * tok)
        queries = nn(y_tok, mext[3 * h]).astype(BF16)
        q_rows = nt(queries, mext[3 * h + 1]) * root_scale
        lq[here, :] = split_const(q_rows, later_keys, q_rows[:, ONE_A : ONE_A + 1])

    def project_keys(h):
        here = slice(h * tok, (h + 1) * tok)
        keys = nn(y_tok, mext[3 * h + 1]).astype(BF16)
        values = nn(y_tok, mext[3 * h + 2]).astype(BF16)
        k_rows = nt(keys, mext[3 * h]) * root_scale
        minus_totals = jnp.where((side_lane == h) | (side_lane == heads + h), -1.0, 0.0).astype(BF16)
        lk[here, :] = jnp.concatenate(
            [split_const(k_rows, earlier_queries, k_rows[:, ONE_A : ONE_A + 1]), minus_totals], axis=1
        )
        v_rows = jnp.concatenate([nt(values, wo[h]), jnp.zeros((tok, SIDE), F32)], axis=1)
        lv[here, :] = jnp.where(zlane == channels + 2 * heads + h, -1.0, v_rows).astype(BF16)

    def chunk_of(buffer, c):
        return jnp.concatenate([buffer[c * per_chunk + i] for i in range(per_chunk)], axis=1)

    def attend(first, end):
        rows = slice(first * tok, end * tok)
        mx[rows, :] = jnp.full((rows.stop - rows.start, tok), masked_value, F32)

        def score_step(c, carry):
            scores = nn(lq[rows, :], chunk_of(slabs, c))
            s_ref[c, rows, :] = scores
            best = mx[rows, :]
            for i in range(per_chunk):
                best = jnp.maximum(best, scores[:, i * tok : (i + 1) * tok])
            mx[rows, :] = best
            return carry

        lax.fori_loop(0, chunks, score_step, 0)
        top = jnp.max(mx[rows, :], axis=1, keepdims=True)
        mx[rows, :] = jnp.broadcast_to(top, (rows.stop - rows.start, tok))
        t1[rows, :] = jnp.zeros((rows.stop - rows.start, ROWS), F32)

        def value_step(c, carry):
            best = mx[rows, :]
            weights = jnp.exp2(s_ref[c, rows, :] - jnp.concatenate([best] * per_chunk, axis=1)).astype(BF16)
            p_ref[c, rows, :] = weights
            t1[rows, :] += nt(weights, chunk_of(slabs, c))
            return carry

        lax.fori_loop(0, chunks, value_step, 0)
        totals = t1[rows, ONE_A : ONE_A + 1]
        t1[rows, :] = t1[rows, :] * (1.0 / totals)
        mx[rows, :] = jnp.where(iota((rows.stop - rows.start, tok), 1) == 0, mx[rows, :], totals)

    def velocity_terms(first, end):
        terms = jnp.zeros((channels, tok), F32)
        for h in range(first, end):
            attended = nn(t1[h * tok : (h + 1) * tok, :].astype(BF16), mext[3 * h + 2]).astype(BF16)
            terms = terms + nt(wo[h], attended)
        return terms

    split = 2
    for b in range(3 * split):
        ag_wait(b)
        extend(b)
    for h in range(split):
        project(h)
    attend(0, split)
    terms = velocity_terms(0, split)
    for b in range(3 * split, last):
        ag_wait(b)
        extend(b)
    for h in range(split, heads):
        project(h)
    attend(split, heads)
    terms = terms + velocity_terms(split, heads)

    vb[tp] = terms.astype(BF16)

    def term_copy(d):
        other = lax.rem(tp + d, tp_count)
        return pltpu.make_async_remote_copy(
            src_ref=vb.at[tp], dst_ref=vb.at[tp], send_sem=v_send.at[other], recv_sem=v_recv.at[tp],
            device_id={"tp": other}, device_id_type=MESH,
        )

    def term_arrival(d):
        other = lax.rem(tp + d, tp_count)
        return pltpu.make_async_remote_copy(
            src_ref=vb.at[other], dst_ref=vb.at[other], send_sem=v_send.at[other], recv_sem=v_recv.at[other],
            device_id={"tp": other}, device_id_type=MESH,
        )

    def role_copy(d):
        slot = (role - 1) * tp_count + tp
        other = lax.rem(tp + d, tp_count)
        return pltpu.make_async_remote_copy(
            src_ref=vb.at[tp], dst_ref=xb.at[slot], send_sem=x_send.at[other], recv_sem=x_recv.at[slot],
            device_id={"role": 0, "tp": other}, device_id_type=MESH,
        )

    @pl.when(role != 0)
    def _():
        for d in (2, 1, 3, 0):
            role_copy(d).start()

    for d in (2, 1, 3):
        term_copy(d).start()

    @pl.when((role == 0) | (role == 3))
    def _():
        for h in range(heads):
            project_keys(h)
        uk[...] = jnp.zeros(uk.shape, F32)
        uv[...] = jnp.zeros(uv.shape, F32)
        u1[...] = jnp.zeros(u1.shape, F32)

    for d in (1, 3, 2):
        term_arrival(d).wait_recv()
    velocity = vb[0].astype(F32)
    for t in range(1, tp_count):
        velocity = velocity + vb[t].astype(F32)
    velocity = velocity.astype(BF16)
    vel[...] = velocity

    def other_velocity(r):
        value = xb[(r - 1) * tp_count].astype(F32)
        for t in range(1, tp_count):
            value = value + xb[(r - 1) * tp_count + t].astype(F32)
        return value.astype(BF16).astype(F32)

    @pl.when(role == 0)
    def _():
        for i in range(3 * tp_count):
            pltpu.make_async_remote_copy(
                src_ref=xb.at[i], dst_ref=xb.at[i], send_sem=x_send.at[0], recv_sem=x_recv.at[i],
                device_id={"tp": lax.rem(tp + 1, tp_count)}, device_id_type=MESH,
            ).wait_recv()
        with_prompt, without_prompt = other_velocity(1), other_velocity(2)
        real = without_prompt + guide_scale * (with_prompt - without_prompt)
        real_clean = noised.astype(F32) - sigma * real
        fake_clean = noised.astype(F32) - sigma * other_velocity(3)
        cot_ref[0:64, :] = fake_clean - real_clean
        dist = jnp.sum(jnp.abs(clean32 - real_clean), keepdims=True)
        cot_ref[64:72, :] = jnp.broadcast_to(dist, (8, tok))

    @pl.when(role == 3)
    def _():
        cot_ref[0:64, :] = velocity.astype(F32) - (fresh32 - clean32)
        cot_ref[64:72, :] = jnp.zeros((8, tok), F32)

    def backward():
        cot = cot_ref[0:64, :]
        zc[me] = cot.astype(BF16)
        zc_start()
        cot_tok = jnp.transpose(cot).astype(BF16)
        side = iota((tok, tok), 1)
        columns = jnp.broadcast_to(cot_ref[64:65, 0:1], (tok, tok))
        for h in range(heads):
            here = slice(h * tok, (h + 1) * tok)
            grad_attended = nn(cot_tok, wo[h]).astype(BF16)
            g_rows = nt(grad_attended, mext[3 * h + 2])
            const = g_rows[:, ONE_A : ONE_A + 1]
            g_now = jnp.where(lane < ONE_A, g_rows, 0.0).astype(BF16)
            inner = jnp.sum(g_now.astype(F32) * t1[here, :], axis=1, keepdims=True)
            lg[here, :] = split_const(g_now.astype(F32), 0.0, -inner)
            log_total = mx[here, 0:1] + jnp.log2(mx[here, 1:2])
            log_high = log_total.astype(BF16).astype(F32)
            columns = jnp.where(side == h, log_high, columns)
            columns = jnp.where(side == heads + h, log_total - log_high, columns)
            columns = jnp.where(side == 2 * heads + h, inner + const, columns)
        zl[me] = jnp.transpose(columns)[0:SIDE].astype(BF16)
        zl_start()

        def query_step(c, carry):
            there = chunk_of(slabs, c)
            centred = nn(lg[...], there)
            grad_scores = (p_ref[c].astype(F32) * centred).astype(BF16)
            u1[...] += nt(grad_scores, there)
            return carry

        lax.fori_loop(0, chunks, query_step, 0)

        def key_step(c, carry):
            whos = [far_first(seq_count - 1 - per_chunk * c - i) for i in range(per_chunk)]

            @pl.when(c > 0)
            def _():
                zc_wait_from(whos[0])
                zl_wait_from(whos[0])

            for who in whos[1:]:
                zc_wait_from(who)
                zl_wait_from(who)
            there = jnp.concatenate([slabs[who] for who in whos], axis=1)
            cots = jnp.concatenate([zc[who] for who in whos], axis=1)
            sides = jnp.concatenate([zl[who] for who in whos], axis=1)
            probs = jnp.exp2(nn(lk[...], jnp.concatenate([there, sides], axis=0)))
            centred = nn(lv[...], jnp.concatenate([cots, sides], axis=0))
            uk[...] += nt((probs * centred).astype(BF16), there)
            uv[...] += nt(probs.astype(BF16), cots)
            return carry

        lax.fori_loop(0, chunks, key_step, 0)
        distance = jnp.zeros((1, tok), F32)
        for s in range(seq_count):
            distance = distance + zl[s].astype(F32)[SIDE - 1 : SIDE]
        spread = distance / (every * channels) + eps_norm
        factor = jnp.where(role == 0, 1.0 / spread, 1.0)
        for h in range(heads):
            here = slice(h * tok, (h + 1) * tok)
            rows_q = (u1[here, :] * (inv_root / mx[here, 1:2])).astype(BF16)
            grads[h, 0] = (nn(rows_q, mext[3 * h + 1]) * factor).astype(BF16)
            rows_k = (uk[here, :] * inv_root).astype(BF16)
            grads[h, 1] = (nn(rows_k, mext[3 * h]) * factor).astype(BF16)
            grads[h, 2] = (nn(uv[here, :].astype(BF16), wo[h]) * factor).astype(BF16)
        zc_wait_sent()
        zl_wait_sent()

    @pl.when((role == 0) | (role == 3))
    def _():
        backward()

    @pl.when((role != 0) & (role != 3))
    def _():
        grads[...] = jnp.zeros(grads.shape, BF16)

    y_wait_sent()

    def sent_step(k, carry):
        who = far_first(k)
        by_length(block_at(who) == last, lambda rows: rs_copy(who, rows).wait_send())
        by_length(my_block == last, lambda rows: ag_copy(who, rows).wait_send())
        return carry

    lax.fori_loop(0, seq_count - 1, sent_step, 0)
    for d in range(1, tp_count):
        quarter_copy(d).wait_send()
        term_copy(d).wait_send()

    @pl.when(role != 0)
    def _():
        for d in range(tp_count):
            role_copy(d).wait_send()


def solution(mesh):
    seq_count, tp_count = mesh.shape["seq"], mesh.shape["tp"]
    x_hi = 2

    def on_device(gen_input, generated, noise, timesteps, block_lengths, w_embed, w_qkv, w_out, modulation):
        tok, channels = gen_input.shape
        feats, heads, _, head = w_qkv.shape[1:]
        rows = heads * tok
        chunk = 2 * tok
        chunks = seq_count * tok // chunk
        vmem = pl.BlockSpec(memory_space=pltpu.VMEM)
        hbm = pl.BlockSpec(memory_space=pltpu.HBM)
        dma = pltpu.SemaphoreType.DMA
        velocity, grads = pl.pallas_call(
            functools.partial(kernel, seq_count, tp_count, x_hi),
            out_shape=(
                jax.ShapeDtypeStruct((channels, tok), BF16),
                jax.ShapeDtypeStruct((heads, 3, tok, head), BF16),
            ),
            in_specs=[hbm] * 9,
            out_specs=(vmem, vmem),
            scratch_shapes=[
                pltpu.VMEM((channels, tok), BF16),
                pltpu.VMEM((channels, tok), BF16),
                pltpu.VMEM((channels, tok), BF16),
                pltpu.SMEM(timesteps.shape, jnp.int32),
                pltpu.SMEM(block_lengths.shape, jnp.int32),
                pltpu.VMEM((2, feats + 64), F32),
                pltpu.VMEM((channels, feats), BF16),
                pltpu.VMEM((heads, 3, feats, head), BF16),
                pltpu.VMEM((heads, channels, head), BF16),
                pltpu.VMEM((160, feats), BF16),
                pltpu.VMEM((seq_count, 80, 128), BF16),
                pltpu.VMEM((seq_count, 80, 128), BF16),
                pltpu.VMEM((seq_count, 80, 128), BF16),
                pltpu.VMEM((tp_count, channels // tp_count, tok), BF16),
                pltpu.VMEM((tp_count, seq_count, channels // tp_count, tok), BF16),
                pltpu.VMEM((seq_count, ROWS, tok), BF16),
                pltpu.VMEM((3 * heads, ROWS, head), BF16),
                pltpu.VMEM((rows, ROWS), BF16),
                pltpu.VMEM((rows, ROWS + SIDE), BF16),
                pltpu.VMEM((rows, channels + SIDE), BF16),
                pltpu.VMEM((rows, ROWS), BF16),
                pltpu.VMEM((chunks, rows, chunk), F32),
                pltpu.VMEM((chunks, rows, chunk), BF16),
                pltpu.VMEM((rows, ROWS), F32),
                pltpu.VMEM((rows, ROWS), F32),
                pltpu.VMEM((rows, ROWS), F32),
                pltpu.VMEM((rows, channels), F32),
                pltpu.VMEM((rows, tok), F32),
                pltpu.VMEM((tp_count, channels, tok), BF16),
                pltpu.VMEM((3 * tp_count, channels, tok), BF16),
                pltpu.VMEM((seq_count, channels, tok), BF16),
                pltpu.VMEM((seq_count, SIDE, tok), BF16),
                pltpu.VMEM((channels + 8, tok), F32),
                dma((9,)),
                dma((seq_count,)), dma((seq_count,)),
                dma((tp_count,)), dma((tp_count,)),
                dma((seq_count,)), dma((seq_count,)),
                dma((seq_count,)), dma((seq_count,)),
                dma((seq_count,)), dma((seq_count,)),
                dma((seq_count,)), dma((seq_count,)),
                dma((tp_count,)), dma((tp_count,)),
                dma((tp_count,)), dma((3 * tp_count,)),
            ],
            compiler_params=pltpu.CompilerParams(
                collective_id=0, has_side_effects=True, vmem_limit_bytes=62 * 1024 * 1024
            ),
            name="distill",
        )(
            gen_input.T,
            generated.T,
            noise.T,
            timesteps,
            block_lengths,
            jnp.transpose(w_embed, (0, 2, 1)),
            jnp.transpose(w_qkv, (0, 2, 3, 1, 4)),
            jnp.transpose(w_out, (0, 1, 3, 2)),
            modulation[0],
        )
        return (velocity.T[None], jnp.transpose(grads, (2, 0, 1, 3))[None])

    placed = (
        P("seq", None),
        P("seq", None),
        P("seq", None),
        P(),
        P(),
        P(None, "seq", None),
        P(None, "seq", "tp", None, None),
        P(None, "tp", None, None),
        P("role", None, None),
    )
    return jax.shard_map(
        on_device,
        mesh=mesh,
        in_specs=placed,
        out_specs=(P("role", "seq", None), P("role", "seq", "tp", None, None)),
        check_vma=False,
    )
```

```python
import functools
import math

import jax
import jax.numpy as jnp
from jax import lax
from jax.experimental import pallas as pl
from jax.experimental.pallas import tpu as pltpu
from jax.sharding import PartitionSpec as P

MESH = pl.DeviceIdType.MESH
F32 = jnp.float32
BF16 = jnp.bfloat16

eps_norm = 1e-06
masked_value = -1e30
guide_scale = 5.0

ROWS = 144
MAIN = 80
ONE_A = 64
MARK = 65
ONE_B = 72
SIDE = 16


def nn(a, b):
    return lax.dot_general(a, b, (((1,), (0,)), ((), ())), preferred_element_type=F32)


def nt(a, b):
    return lax.dot_general(a, b, (((1,), (1,)), ((), ())), preferred_element_type=F32)


def iota(shape, dim):
    return lax.broadcasted_iota(jnp.int32, shape, dim)


def kernel(
    seq_count, tp_count, x_hi,
    gen_hbm, clean_hbm, fresh_hbm, steps_hbm, lens_hbm, emb_hbm, qkv_hbm, out_hbm, mod_hbm,
    vel, grads,
    gen, clean, fresh, steps, lens, mod, emb, wq, wo, lhs, part, rs, mall, ylocal, ybuf, slabs, mext,
    lq, lk, lv, lg, s_ref, p_ref, t1, u1, uk, uv, mx, vb, xb, zb, zl, pt_ref, gq, cot_ref, term_ref,
    load_sem, y_send, y_recv, w_send, w_recv, rs_send, rs_recv, ag_send, ag_recv,
    z_send, z_recv, zl_send, zl_recv, v_send, v_recv, x_send, x_recv,
):
    role = lax.axis_index("role")
    me = lax.axis_index("seq")
    tp = lax.axis_index("tp")
    channels, tok = gen.shape
    feats = emb.shape[1]
    heads, _, head = wo.shape
    blocks = lens.shape[0]
    every = seq_count * tok
    net = lax.div(role + 1, 2)
    per_chunk = s_ref.shape[2] // tok
    chunks = seq_count // per_chunk
    z_len = seq_count // x_hi
    my_x, my_z = lax.div(me, z_len), lax.rem(me, z_len)
    last = 3 * heads

    x_at = [lax.rem(my_x + dx, x_hi) * z_len for dx in range(x_hi)]
    z_at = [lax.rem(my_z + dz, z_len) for dz in range(z_len)]
    far_z = [4, 3, 5, 2, 6, 1, 7, 0]
    far_first = [x_at[dx] + z_at[dz] for dz in far_z for dx in (1, 0)][:-1]
    ring_first = [x_at[dx] + z_at[dz] for dx in (0, 1) for dz in far_z]
    self_in_ring = z_len - 1

    owner_order = [x * z_len + z for tier in ((0, 2, 4, 6), (1, 5), (3, 7)) for x in range(x_hi) for z in tier]
    last_owner = owner_order[0]
    block_owner = owner_order[1:] + [last_owner]

    def greeted_in_tiers():
        parity = lax.rem(my_z, 2)
        out = []
        for i in (2, 1, 3, 0):
            z = lax.rem(my_z + parity + 2 * i, z_len)
            out += [(x_at[1] + z, False), (x_at[0] + z, i == 0)]
        for residue in (1, 3):
            first = lax.rem(residue + z_len - my_z, 4)
            for step in (4, 0):
                z = lax.rem(my_z + first + step, z_len)
                out += [(x_at[1] + z, False), (x_at[0] + z, step == 0)]
        return out

    barrier = pltpu.get_barrier_semaphore()

    for who in far_first:
        pl.semaphore_signal(barrier, inc=1, device_id={"seq": who}, device_id_type=MESH)
    for d in range(1, tp_count):
        pl.semaphore_signal(barrier, inc=1, device_id={"tp": lax.rem(tp + d, tp_count)}, device_id_type=MESH)

    @pl.when(role == 0)
    def _():
        for other in range(1, 4):
            for t in range(tp_count):
                pl.semaphore_signal(barrier, inc=1, device_id={"role": other, "tp": t}, device_id_type=MESH)

    feat_start = pl.multiple_of(lax.div(me * feats, 128) * 128, 128)
    sources = (
        (emb_hbm.at[net], emb), (mod_hbm.at[:, pl.ds(feat_start, mod.shape[1])], mod), (steps_hbm, steps), (lens_hbm, lens),
        (gen_hbm, gen), (clean_hbm, clean), (fresh_hbm, fresh), (qkv_hbm.at[net], wq), (out_hbm.at[net], wo),
    )
    loads = [pltpu.make_async_copy(src, dst, load_sem.at[i]) for i, (src, dst) in enumerate(sources)]
    for load in loads:
        load.start()
    for load in loads[2:7]:
        load.wait()

    ends = []
    total = jnp.int32(0)
    for j in range(blocks):
        total = total + lens[j]
        ends.append(total)

    def block_of(positions):
        ids = jnp.zeros_like(positions)
        for j in range(blocks):
            ids = ids + (positions >= ends[j]).astype(jnp.int32)
        return ids

    lane_block = block_of(me * tok + iota((1, tok), 1))
    sigma = jnp.zeros((1, tok), F32)
    for j in range(blocks):
        sigma = sigma + jnp.where(lane_block == j, steps[j].astype(F32), 0.0)
    sigma = sigma / 1000.0
    clean32 = clean[...].astype(F32)
    fresh32 = fresh[...].astype(F32)
    noised = ((1.0 - sigma) * clean32 + sigma * fresh32).astype(BF16)
    latents = jnp.where(role == 0, gen[...].astype(F32), noised.astype(F32)).astype(BF16)
    quarter = channels // tp_count
    for t in range(tp_count):
        ylocal[t] = latents[t * quarter : (t + 1) * quarter]
    ybuf[tp, me] = ylocal[tp]

    loads[0].wait()
    loads[1].wait()
    odd = lax.rem(me, 2) == 1
    window = mod[...]
    mine = jnp.where(odd, window[:, 64 : 64 + feats], window[:, :feats])
    scale, shift = 1.0 + mine[0:1], mine[1:2]
    emb_now = emb[...]
    scaled = emb_now.astype(F32) * scale
    scaled_hi = scaled.astype(BF16)
    shift_rows = jnp.where(iota((16, feats), 0) == 0, shift, 0.0)
    shift_hi = shift_rows.astype(BF16)
    lhs[0:64, :] = scaled_hi
    lhs[64:80, :] = shift_hi
    lhs[80:144, :] = (scaled - scaled_hi.astype(F32)).astype(BF16)
    lhs[144:160, :] = (shift_rows - shift_hi.astype(F32)).astype(BF16)
    gram = nt(emb_now, jnp.concatenate([emb_now, emb_now], axis=0))
    gram_hi = gram.astype(BF16).astype(F32)
    left_half = iota((channels, 2 * channels), 1) < channels
    part[last_owner, 0:64, :] = jnp.where(left_half, gram_hi, gram - gram_hi).astype(BF16)
    loads[7].wait()
    lhs_now = lhs[...]
    bias = jnp.zeros((16, head), F32)
    bias_row = iota((16, head), 0)
    for b in range(last):
        both = nn(lhs_now, wq[b % heads, b // heads])
        both = both[0:80] + both[80:160]
        part[block_owner[b], 0:64, :] = both[0:64].astype(BF16)
        bias = jnp.where(bias_row == b, both[64:65], bias)
    part[last_owner, 64:80, :] = bias.astype(BF16)
    rs[me, 0:64, :] = part[me, 0:64, :]

    @pl.when(me == last_owner)
    def _():
        rs[last_owner, 64:80, :] = part[last_owner, 64:80, :]

    @pl.when(role == 0)
    def _():
        pl.semaphore_wait(barrier, seq_count - 1 + tp_count - 1)

    @pl.when(role != 0)
    def _():
        pl.semaphore_wait(barrier, seq_count - 1 + tp_count - 1 + tp_count)

    def over_seq(src, dst, send, recv, order):
        def copy(who):
            return pltpu.make_async_remote_copy(
                src_ref=src, dst_ref=dst(me), send_sem=send.at[who], recv_sem=recv.at[me],
                device_id={"seq": who}, device_id_type=MESH,
            )

        def start():
            for who in order:
                copy(who).start()

        def wait_sent():
            for who in order:
                copy(who).wait_send()

        def wait_from(whos):
            for who in whos:
                pltpu.make_async_remote_copy(
                    src_ref=dst(who), dst_ref=dst(who), send_sem=send.at[who], recv_sem=recv.at[who],
                    device_id={"seq": who}, device_id_type=MESH,
                ).wait_recv()

        return start, wait_sent, wait_from

    ring_others = ring_first[:self_in_ring] + ring_first[self_in_ring + 1 :]
    y_start, y_wait_sent, y_wait_from = over_seq(ybuf.at[tp, me], lambda who: ybuf.at[tp, who], y_send, y_recv, far_first)
    zl_start, zl_wait_sent, zl_wait_from = over_seq(zl.at[me], lambda who: zl.at[who], zl_send, zl_recv, far_first)
    z_start, z_wait_sent, z_wait_from = over_seq(zb.at[me], lambda who: zb.at[who], z_send, z_recv, far_first)

    def rs_copy(who, rows):
        return pltpu.make_async_remote_copy(
            src_ref=part.at[who, 0:rows], dst_ref=rs.at[me, 0:rows], send_sem=rs_send.at[who],
            recv_sem=rs_recv.at[me], device_id={"seq": who}, device_id_type=MESH,
        )

    def rs_arrival(who, rows):
        return pltpu.make_async_remote_copy(
            src_ref=rs.at[who, 0:rows], dst_ref=rs.at[who, 0:rows], send_sem=rs_send.at[who],
            recv_sem=rs_recv.at[who], device_id={"seq": who}, device_id_type=MESH,
        )

    def ag_copy(who, rows):
        mine = mall.at[me, 0:rows]
        return pltpu.make_async_remote_copy(
            src_ref=mine, dst_ref=mine, send_sem=ag_send.at[who], recv_sem=ag_recv.at[me],
            device_id={"seq": who}, device_id_type=MESH,
        )

    long_rows, short_rows = channels + 16, channels

    def by_length(is_long, action):
        @pl.when(is_long)
        def _():
            action(long_rows)

        @pl.when(jnp.logical_not(is_long))
        def _():
            action(short_rows)

    def ag_wait(b):
        owner = block_owner[b]
        there = mall.at[owner, 0 : long_rows if b == last else short_rows]

        @pl.when(me != owner)
        def _():
            pltpu.make_async_remote_copy(
                src_ref=there, dst_ref=there, send_sem=ag_send.at[owner], recv_sem=ag_recv.at[owner],
                device_id={"seq": owner}, device_id_type=MESH,
            ).wait_recv()

    for who, may_be_me in greeted_in_tiers():

        def send(who=who):
            by_length(who == last_owner, lambda rows: rs_copy(who, rows).start())

        if may_be_me:
            pl.when(who != me)(send)
        else:
            send()

    y_start()

    row_id = iota((16, every), 0)
    wide_block = block_of(iota((1, every), 1))
    extras = jnp.where(
        (row_id == 0) | (row_id == ONE_B - ONE_A) | ((row_id < ONE_B - ONE_A) & (wide_block == row_id - 1)), 1.0, 0.0
    ).astype(BF16)
    for s in range(seq_count):
        slabs[s, 64:80, :] = extras[:, s * tok : (s + 1) * tok]

    def rs_wait(rows):
        for who in far_first:
            rs_arrival(who, rows).wait_recv()

    by_length(me == last_owner, rs_wait)
    owned = jnp.zeros((64, 128), F32)
    for s in range(seq_count):
        owned = owned + rs[s, 0:64, :].astype(F32)
    folded = owned + pltpu.roll(owned, 64, 1)
    folded_hi = folded.astype(BF16).astype(F32)
    half = jnp.where(left_half, folded_hi, folded - folded_hi)
    mall[me, 0:64, :] = jnp.where(me == last_owner, half, owned).astype(BF16)

    @pl.when(me == last_owner)
    def _():
        owned_bias = jnp.zeros((16, 128), F32)
        for s in range(seq_count):
            owned_bias = owned_bias + rs[s, 64:80, :].astype(F32)
        mall[last_owner, 64:80, :] = owned_bias.astype(BF16)

    def ag_start(rows):
        for who in far_first:
            ag_copy(who, rows).start()

    by_length(me == last_owner, ag_start)

    y_wait_from(far_first)

    def quarter_copy(d):
        other = lax.rem(tp + d, tp_count)
        return pltpu.make_async_remote_copy(
            src_ref=ybuf.at[tp], dst_ref=ybuf.at[tp], send_sem=w_send.at[other], recv_sem=w_recv.at[tp],
            device_id={"tp": other}, device_id_type=MESH,
        )

    def quarter_arrival(d):
        other = lax.rem(tp + d, tp_count)
        return pltpu.make_async_remote_copy(
            src_ref=ybuf.at[other], dst_ref=ybuf.at[other], send_sem=w_send.at[other], recv_sem=w_recv.at[other],
            device_id={"tp": other}, device_id_type=MESH,
        )

    for d in (2, 1, 3):
        quarter_copy(d).start()

    for d in (2, 1, 3):
        quarter_arrival(d).wait_recv()
    ag_wait(last)
    y_all = jnp.concatenate(
        [jnp.concatenate([ybuf[t, s] for t in range(tp_count)], axis=0) for s in range(seq_count)], axis=1
    )
    y_wide = y_all.astype(F32)
    gram_y = nn(mall[last_owner, 0:64, :], jnp.concatenate([y_all, y_all], axis=0))
    mean_square = jnp.sum(gram_y * y_wide, axis=0, keepdims=True) / (feats * seq_count)
    ry = y_wide * lax.rsqrt(jnp.maximum(mean_square, 0.0) + eps_norm)
    ry_hi = ry.astype(BF16)
    ry_lo = (ry - ry_hi.astype(F32)).astype(BF16)
    for s in range(seq_count):
        slabs[s, 0:64, :] = ry_hi[:, s * tok : (s + 1) * tok]
        slabs[s, 80:144, :] = ry_lo[:, s * tok : (s + 1) * tok]

    loads[8].wait()
    y_tok = jnp.transpose(slabs[me].astype(F32)).astype(BF16)
    tok_block = block_of(me * tok + iota((tok, ROWS), 0))
    lane = iota((tok, ROWS), 1)
    in_marks = (lane >= MARK) & (lane < MARK + blocks)
    later_keys = jnp.where(in_marks & (lane - MARK > tok_block), masked_value, 0.0)
    earlier_queries = jnp.where(in_marks & (lane - MARK < tok_block), masked_value, 0.0)
    root_scale = math.log2(math.e) / math.sqrt(head)
    inv_root = 1.0 / math.sqrt(head)
    first_row = iota((16, head), 0) == 0
    zlane = iota((tok, channels + SIDE), 1)
    side_lane = iota((tok, SIDE), 1)

    def split_const(rows, extra, const):
        low = const - const.astype(BF16).astype(F32)
        at = iota(rows.shape, 1)
        return jnp.where(at == ONE_B, low, jnp.where(at == ONE_A, const, rows + extra)).astype(BF16)

    def extend(b):
        mext[b, 0:64, :] = mall[block_owner[b], 0:64, :]
        mext[b, 80:144, :] = mall[block_owner[b], 0:64, :]
        mext[b, 64:80, :] = jnp.where(first_row, mall[last_owner, 64:80, :].astype(F32)[b : b + 1], 0.0).astype(BF16)

    def project(h):
        here = slice(h * tok, (h + 1) * tok)
        queries = nn(y_tok, mext[h]).astype(BF16)
        q_rows = nt(queries, mext[heads + h]) * root_scale
        lq[here, :] = split_const(q_rows, later_keys, q_rows[:, ONE_A : ONE_A + 1])

    def project_keys(h):
        here = slice(h * tok, (h + 1) * tok)
        keys = nn(y_tok, mext[heads + h]).astype(BF16)
        values = nn(y_tok, mext[2 * heads + h]).astype(BF16)
        k_rows = nt(keys, mext[h]) * root_scale
        minus_totals = jnp.where((side_lane == h) | (side_lane == heads + h), -1.0, 0.0).astype(BF16)
        lk[here, :] = jnp.concatenate(
            [split_const(k_rows, earlier_queries, k_rows[:, ONE_A : ONE_A + 1]), minus_totals], axis=1
        )
        v_rows = jnp.concatenate([nt(values, wo[h]), jnp.zeros((tok, SIDE), F32)], axis=1)
        lv[here, :] = jnp.where(zlane == channels + h, -1.0, v_rows).astype(BF16)

    def chunk_of(buffer, c):
        return jnp.concatenate([buffer[c * per_chunk + i] for i in range(per_chunk)], axis=1)

    def attend(first, end):
        rows = slice(first * tok, end * tok)
        mx[rows, :] = jnp.full((rows.stop - rows.start, tok), masked_value, F32)

        def score_step(c):
            scores = nn(lq[rows, :], chunk_of(slabs, c))
            s_ref[c, rows, :] = scores
            best = mx[rows, :]
            for i in range(per_chunk):
                best = jnp.maximum(best, scores[:, i * tok : (i + 1) * tok])
            mx[rows, :] = best

        for c in range(chunks):
            score_step(c)
        top = jnp.max(mx[rows, :], axis=1, keepdims=True)
        mx[rows, :] = jnp.broadcast_to(top, (rows.stop - rows.start, tok))
        t1[rows, :] = jnp.zeros((rows.stop - rows.start, MAIN), F32)

        def value_step(c):
            best = mx[rows, :]
            weights = jnp.exp2(s_ref[c, rows, :] - jnp.concatenate([best] * per_chunk, axis=1)).astype(BF16)
            p_ref[c, rows, :] = weights
            t1[rows, :] += nt(weights, chunk_of(slabs, c)[0:MAIN])

        for c in range(chunks):
            value_step(c)
        totals = t1[rows, ONE_A : ONE_A + 1]
        t1[rows, :] = t1[rows, :] * (1.0 / totals)
        mx[rows, :] = jnp.where(iota((rows.stop - rows.start, tok), 1) == 0, mx[rows, :], totals)

    def velocity_terms(first, end):
        terms = jnp.zeros((channels, tok), F32)
        for h in range(first, end):
            attended = nn(t1[h * tok : (h + 1) * tok, :].astype(BF16), mext[2 * heads + h, 0:MAIN, :]).astype(BF16)
            term = nt(wo[h], attended)
            term_ref[h] = term
            terms = terms + term
        return terms

    for b in range(2 * heads):
        ag_wait(b)
        extend(b)
    for h in range(heads):
        project(h)
    attend(0, heads)
    for b in range(2 * heads, last):
        ag_wait(b)
        extend(b)
    terms = velocity_terms(0, heads)

    vb[tp] = terms.astype(BF16)

    def term_copy(d):
        other = lax.rem(tp + d, tp_count)
        return pltpu.make_async_remote_copy(
            src_ref=vb.at[tp], dst_ref=vb.at[tp], send_sem=v_send.at[other], recv_sem=v_recv.at[tp],
            device_id={"tp": other}, device_id_type=MESH,
        )

    def term_arrival(d):
        other = lax.rem(tp + d, tp_count)
        return pltpu.make_async_remote_copy(
            src_ref=vb.at[other], dst_ref=vb.at[other], send_sem=v_send.at[other], recv_sem=v_recv.at[other],
            device_id={"tp": other}, device_id_type=MESH,
        )

    def role_copy(d):
        slot = (role - 1) * tp_count + tp
        other = lax.rem(tp + d, tp_count)
        return pltpu.make_async_remote_copy(
            src_ref=vb.at[tp], dst_ref=xb.at[slot], send_sem=x_send.at[other], recv_sem=x_recv.at[slot],
            device_id={"role": 0, "tp": other}, device_id_type=MESH,
        )

    @pl.when(role != 0)
    def _():
        for d in (2, 1, 3, 0):
            role_copy(d).start()

        for d in (2, 1, 3):
            term_copy(d).start()

    @pl.when((role == 0) | (role == 3))
    def _():
        side = iota((tok, tok), 1)
        columns = jnp.zeros((tok, tok), F32)
        for h in range(heads):
            here = slice(h * tok, (h + 1) * tok)
            log_total = mx[here, 0:1] + jnp.log2(mx[here, 1:2])
            log_high = log_total.astype(BF16).astype(F32)
            columns = jnp.where(side == h, log_high, jnp.where(side == heads + h, log_total - log_high, columns))
        zl[me] = jnp.transpose(columns)[0:SIDE].astype(BF16)
        zl_start()
        for h in range(heads):
            project_keys(h)
        uk[...] = jnp.zeros(uk.shape, F32)
        uv[...] = jnp.zeros(uv.shape, F32)
        u1[...] = jnp.zeros(u1.shape, F32)

    y_wait_sent()

    for who in far_first:
        by_length(who == last_owner, lambda rows: rs_copy(who, rows).wait_send())

    def ag_sent(rows):
        for who in far_first:
            ag_copy(who, rows).wait_send()

    by_length(me == last_owner, ag_sent)
    for d in range(1, tp_count):
        quarter_copy(d).wait_send()

    def other_velocity(r):
        value = xb[(r - 1) * tp_count].astype(F32)
        for t in range(1, tp_count):
            value = value + xb[(r - 1) * tp_count + t].astype(F32)
        return value.astype(BF16).astype(F32)

    def own_velocity():
        for d in (1, 3, 2):
            term_arrival(d).wait_recv()
        value = vb[0].astype(F32)
        for t in range(1, tp_count):
            value = value + vb[t].astype(F32)
        vel[...] = value.astype(BF16)
        for d in range(1, tp_count):
            term_copy(d).wait_send()

    @pl.when(role != 0)
    def _():
        own_velocity()
        for d in range(tp_count):
            role_copy(d).wait_send()

    @pl.when(role == 0)
    def _():
        for i in range(3 * tp_count):
            pltpu.make_async_remote_copy(
                src_ref=xb.at[i], dst_ref=xb.at[i], send_sem=x_send.at[0], recv_sem=x_recv.at[i],
                device_id={"tp": lax.rem(tp + 1, tp_count)}, device_id_type=MESH,
            ).wait_recv()
        with_prompt, without_prompt = other_velocity(1), other_velocity(2)
        real = without_prompt + guide_scale * (with_prompt - without_prompt)
        real_clean = noised.astype(F32) - sigma * real
        fake_clean = noised.astype(F32) - sigma * other_velocity(3)
        cot_ref[0:64, :] = fake_clean - real_clean
        dist = jnp.sum(jnp.abs(clean32 - real_clean), keepdims=True)
        cot_ref[64:72, :] = jnp.broadcast_to(dist, (8, tok))

    @pl.when(role == 3)
    def _():
        cot_ref[0:64, :] = vel[...].astype(F32) - (fresh32 - clean32)
        cot_ref[64:72, :] = jnp.zeros((8, tok), F32)

    def backward():
        cot = cot_ref[0:64, :]
        cot16 = cot.astype(BF16)
        cot_wide = cot16.astype(F32)
        side_row = iota((SIDE, tok), 0)
        side_rows = jnp.broadcast_to(cot_ref[64:65, :], (SIDE, tok))
        for h in range(heads):
            delta = jnp.sum(cot_wide * term_ref[h], axis=0, keepdims=True)
            side_rows = jnp.where(side_row == h, delta, side_rows)
        zb[me, 0:64, :] = cot16
        zb[me, 64:80, :] = side_rows.astype(BF16)
        z_start()

        @pl.when(role == 0)
        def _():
            for d in (2, 1, 3):
                term_copy(d).start()

        cot_tok = jnp.transpose(cot).astype(BF16)
        for h in range(heads):
            here = slice(h * tok, (h + 1) * tok)
            grad_attended = nn(cot_tok, wo[h]).astype(BF16)
            g_rows = nt(grad_attended, mext[2 * heads + h, 0:MAIN, :])
            g_now = jnp.where(iota((tok, MAIN), 1) < ONE_A, g_rows, 0.0).astype(BF16).astype(F32)
            inner = jnp.sum(g_now * t1[here, :], axis=1, keepdims=True)
            lg[here, :] = split_const(g_now, 0.0, -inner)

        zl_wait_from(far_first)
        zl_wait_sent()

        @pl.when(role == 0)
        def _():
            own_velocity()


        def near_slabs(c):
            return ring_first[per_chunk * c : per_chunk * (c + 1)]

        def prob_step(c):
            whos = near_slabs(c)
            there = jnp.concatenate([slabs[who] for who in whos], axis=1)
            sides = jnp.concatenate([zl[who] for who in whos], axis=1)
            pt_ref[c] = jnp.exp2(nn(lk[...], jnp.concatenate([there, sides], axis=0))).astype(BF16)

        for c in range(chunks):
            prob_step(c)

        def query_step(c):
            there = chunk_of(slabs, c)[0:MAIN]
            centred = nn(lg[...], there)
            grad_scores = (p_ref[c].astype(F32) * centred).astype(BF16)
            u1[...] += nt(grad_scores, there)

        for c in range(chunks):
            query_step(c)
        for h in range(heads):
            here = slice(h * tok, (h + 1) * tok)
            rows_q = (u1[here, :] * (inv_root / mx[here, 1:2])).astype(BF16)
            gq[here, :] = nn(rows_q, mext[heads + h, 0:MAIN, :])

        def key_step(c):
            whos = near_slabs(c)

            there = jnp.concatenate([slabs[who, 0:MAIN, :] for who in whos], axis=1)
            cots = jnp.concatenate([zb[who] for who in whos], axis=1)
            probs = pt_ref[c]
            centred = nn(lv[...], cots)
            uk[...] += nt((probs.astype(F32) * centred).astype(BF16), there)
            uv[...] += nt(probs, cots[0:64])

        z_wait_from(ring_first[:self_in_ring])
        for c in range(chunks // 2):
            key_step(c)
        z_wait_sent()
        z_wait_from(ring_first[self_in_ring + 1 :])
        for c in range(chunks // 2, chunks):
            key_step(c)
        distance = jnp.zeros((1, tok), F32)
        for s in range(seq_count):
            distance = distance + zb[s, 64:80, :].astype(F32)[SIDE - 1 : SIDE]
        spread = distance / (every * channels) + eps_norm
        factor = jnp.where(role == 0, 1.0 / spread, 1.0)
        for h in range(heads):
            here = slice(h * tok, (h + 1) * tok)
            grads[h, 0] = (gq[here, :] * factor).astype(BF16)
            rows_k = (uk[here, :] * inv_root).astype(BF16)
            grads[h, 1] = (nn(rows_k, mext[h, 0:MAIN, :]) * factor).astype(BF16)
            grads[h, 2] = (nn(uv[here, :].astype(BF16), wo[h]) * factor).astype(BF16)


    @pl.when((role == 0) | (role == 3))
    def _():
        backward()

    @pl.when((role != 0) & (role != 3))
    def _():
        grads[...] = jnp.zeros(grads.shape, BF16)


def solution(mesh):
    seq_count, tp_count = mesh.shape["seq"], mesh.shape["tp"]
    x_hi = 2

    def on_device(gen_input, generated, noise, timesteps, block_lengths, w_embed, w_qkv, w_out, modulation):
        tok, channels = gen_input.shape
        feats, heads, _, head = w_qkv.shape[1:]
        rows = heads * tok
        chunk = 4 * tok
        chunks = seq_count * tok // chunk
        vmem = pl.BlockSpec(memory_space=pltpu.VMEM)
        hbm = pl.BlockSpec(memory_space=pltpu.HBM)
        dma = pltpu.SemaphoreType.DMA
        velocity, grads = pl.pallas_call(
            functools.partial(kernel, seq_count, tp_count, x_hi),
            out_shape=(
                pltpu.VMEM((channels, tok), BF16),
                pltpu.VMEM((heads, 3, tok, head), BF16),
            ),
            in_specs=[hbm] * 9,
            out_specs=(vmem, vmem),
            scratch_shapes=[
                pltpu.VMEM((channels, tok), BF16),
                pltpu.VMEM((channels, tok), BF16),
                pltpu.VMEM((channels, tok), BF16),
                pltpu.SMEM(timesteps.shape, jnp.int32),
                pltpu.SMEM(block_lengths.shape, jnp.int32),
                pltpu.VMEM((2, feats + 64), F32),
                pltpu.VMEM((channels, feats), BF16),
                pltpu.VMEM((heads, 3, feats, head), BF16),
                pltpu.VMEM((heads, channels, head), BF16),
                pltpu.VMEM((160, feats), BF16),
                pltpu.VMEM((seq_count, 80, 128), BF16),
                pltpu.VMEM((seq_count, 80, 128), BF16),
                pltpu.VMEM((seq_count, 80, 128), BF16),
                pltpu.VMEM((tp_count, channels // tp_count, tok), BF16),
                pltpu.VMEM((tp_count, seq_count, channels // tp_count, tok), BF16),
                pltpu.VMEM((seq_count, ROWS, tok), BF16),
                pltpu.VMEM((3 * heads, ROWS, head), BF16),
                pltpu.VMEM((rows, ROWS), BF16),
                pltpu.VMEM((rows, ROWS + SIDE), BF16),
                pltpu.VMEM((rows, channels + SIDE), BF16),
                pltpu.VMEM((rows, MAIN), BF16),
                pltpu.VMEM((chunks, rows, chunk), F32),
                pltpu.VMEM((chunks, rows, chunk), BF16),
                pltpu.VMEM((rows, MAIN), F32),
                pltpu.VMEM((rows, MAIN), F32),
                pltpu.VMEM((rows, MAIN), F32),
                pltpu.VMEM((rows, channels), F32),
                pltpu.VMEM((rows, tok), F32),
                pltpu.VMEM((tp_count, channels, tok), BF16),
                pltpu.VMEM((3 * tp_count, channels, tok), BF16),
                pltpu.VMEM((seq_count, channels + SIDE, tok), BF16),
                pltpu.VMEM((seq_count, SIDE, tok), BF16),
                pltpu.VMEM((chunks, rows, chunk), BF16),
                pltpu.VMEM((rows, head), F32),
                pltpu.VMEM((channels + 8, tok), F32),
                pltpu.VMEM((heads, channels, tok), F32),
                dma((9,)),
                dma((seq_count,)), dma((seq_count,)),
                dma((tp_count,)), dma((tp_count,)),
                dma((seq_count,)), dma((seq_count,)),
                dma((seq_count,)), dma((seq_count,)),
                dma((seq_count,)), dma((seq_count,)),
                dma((seq_count,)), dma((seq_count,)),
                dma((tp_count,)), dma((tp_count,)),
                dma((tp_count,)), dma((3 * tp_count,)),
            ],
            compiler_params=pltpu.CompilerParams(
                collective_id=0, has_side_effects=True, vmem_limit_bytes=56 * 1024 * 1024
            ),
            name="distill",
        )(
            gen_input.T,
            generated.T,
            noise.T,
            timesteps,
            block_lengths,
            jnp.transpose(w_embed, (0, 2, 1)),
            jnp.transpose(w_qkv, (0, 2, 3, 1, 4)),
            jnp.transpose(w_out, (0, 1, 3, 2)),
            modulation[0],
        )
        return (velocity.T[None], jnp.transpose(grads, (2, 0, 1, 3))[None])

    placed = (
        P("seq", None),
        P("seq", None),
        P("seq", None),
        P(),
        P(),
        P(None, "seq", None),
        P(None, "seq", "tp", None, None),
        P(None, "tp", None, None),
        P("role", None, None),
    )
    return jax.shard_map(
        on_device,
        mesh=mesh,
        in_specs=placed,
        out_specs=(P("role", "seq", None), P("role", "seq", "tp", None, None)),
        check_vma=False,
    )
```
